32 devices in a mesh: tm: 8 (over z, y), chan: 4 (over x, core).
Axes of the slice: x: 2, y: 2, z: 4, core: 2. Of those that a mesh axis runs over, the one named last changes fastest.
Arguments:
- record: bfloat16 [28672, 10240], P('tm', 'chan'), may hold values from -256 to 256
- pilot_sweep: bfloat16 [3072], replicated, may hold values from -0.109375 to 0.109375
- sweep_table: int32 [3, 8], replicated, may hold values from 0 to 28671, as said below
- owner_map: int32 [2], replicated, may hold values from 0 to 1, each once
Outputs:
- stacks: float32 [2, 1024, 10240], P(None, 'tm', 'chan')
The draws below stay inside these ranges and needn't reach their ends.
Inputs may be any that keep to these rules, and one draw needn't show every extreme that they name: `sweep_table`: column g is sweep g: row 0 lies in [3584 g, 3584 g + 512]; row 1 is its shot, and every shot has at least one sweep; row 2 is the number of earlier sweeps with the same shot.
All inputs are finite; a program needn't handle non-finite values.
Results may differ from the reference program's by a relative error of at most 0.0029.
Values may be sent and summed in bfloat16 or wider, within the bound.
A program may use at most 128 MiB of HBM per device.

```python
import jax
import jax.numpy as jnp
from jax import lax

CHANNELS = 10240
SWEEP = 3072
PILOT_SPACING = 3584
SEG = 1024
ITERS = 3
T_DEV = 3584
TRACE_LENGTH = 28672
SWEEPS = 8
SHOTS = 2
N_TM = 8
N_CHAN = 4


def draw_record(key, part):
    excitation_lines = PILOT_SPACING // 4
    excitation_segments = TRACE_LENGTH // excitation_lines
    position = jnp.arange(TRACE_LENGTH, dtype=jnp.float32) / TRACE_LENGTH
    channel_position = jnp.arange(CHANNELS, dtype=jnp.float32) / CHANNELS
    rough = jax.random.uniform(jax.random.fold_in(key, 3), (CHANNELS,), jnp.float32, 0.0, jnp.log(2.0))
    noise = jax.random.truncated_normal(jax.random.fold_in(key, 1), -4.0, 4.0, (TRACE_LENGTH, CHANNELS), jnp.float32)
    frequency_slope = jnp.exp(jnp.log(3.0) * position)
    single_excitation = jnp.exp(jax.random.uniform(jax.random.fold_in(key, 2), (excitation_segments,), jnp.float32, 0.0, jnp.log(2.0)))
    channel = jnp.exp(jnp.log(3.0) * channel_position + rough)
    cauchy_damping_factor = frequency_slope * jnp.repeat(single_excitation, excitation_lines)
    return (noise * cauchy_damping_factor[:, None] * channel[None, :]).astype(jnp.bfloat16)


def draw_sweep_table(key, part):
    count = SWEEPS
    order_index = jnp.arange(count, dtype=jnp.int32)
    jitter = jax.random.randint(jax.random.fold_in(key, 21), (count,), 0, PILOT_SPACING - SWEEP + 1)
    starts = order_index * PILOT_SPACING + jitter
    first = jax.random.randint(jax.random.fold_in(key, 22), (count,), 0, SHOTS)
    second = jax.random.randint(jax.random.fold_in(key, 23), (count,), 0, SHOTS)
    skewed = jnp.minimum(first, second)
    base = jnp.where(order_index < SHOTS, order_index, skewed)
    labels = base[jax.random.permutation(jax.random.fold_in(key, 24), count)]
    relabel = jax.random.permutation(jax.random.fold_in(key, 25), SHOTS).astype(jnp.int32)
    shots = relabel[labels]
    hits = (shots[:, None] == jnp.arange(SHOTS, dtype=jnp.int32)[None, :]).astype(jnp.int32)
    before = jnp.cumsum(hits, axis=0) - hits
    repeat_shot = jnp.sum(before * hits, axis=1)
    return jnp.stack([starts, shots, repeat_shot]).astype(jnp.int32)


def gaussian(key, dims, scale, bound, held_as=jnp.bfloat16):
    drawn = scale * jax.random.normal(key, dims, jnp.float32)
    return jnp.clip(drawn, min=-bound, max=bound).astype(held_as)


def setup_inputs(seed: int = 0) -> dict:
    key_list = jax.random.split(jax.random.key(seed), 5)
    return {
        "record": draw_record(jax.random.fold_in(key_list[4], 71), 0),
        "pilot_sweep": gaussian(key_list[1], (SWEEP,), SWEEP ** -0.5, 0.109375),
        "sweep_table": draw_sweep_table(jax.random.fold_in(key_list[4], 71), 0),
        "owner_map": jax.random.permutation(key_list[3], SHOTS).astype(jnp.int32),
    }


EPSILON = 1e-6


def reference(record, pilot_sweep, sweep_table, owner_map):
    block_width = CHANNELS // N_CHAN
    width = SEG + SWEEP
    lag_index = jnp.arange(width, dtype=jnp.int32)[None, :] - jnp.arange(SEG, dtype=jnp.int32)[:, None]
    inside = (lag_index >= 0) & (lag_index < SWEEP)
    tapped = pilot_sweep[jnp.clip(lag_index, 0, SWEEP - 1)]
    toeplitz = jnp.where(inside, tapped, jnp.zeros_like(tapped))
    polarity = 1.0 - 2.0 * (sweep_table[2] % 2).astype(jnp.float32)

    def one_sweep(index):
        block_start = index * T_DEV
        first = lax.dynamic_slice_in_dim(record, block_start, T_DEV, 0)
        following = lax.dynamic_slice_in_dim(record, jnp.minimum(index + 1, N_TM - 1) * T_DEV, T_DEV, 0)
        following = jnp.where(index + 1 < N_TM, following, jnp.zeros_like(following))
        joined = jnp.concatenate([first, following], axis=0)
        offset = (sweep_table[0, index] - block_start).astype(jnp.int32)
        window = lax.dynamic_slice_in_dim(joined, offset, width, 0)
        correlation = jnp.dot(toeplitz, window, preferred_element_type=jnp.float32)
        return (correlation * polarity[index]).astype(jnp.bfloat16)

    traces = lax.map(one_sweep, jnp.arange(SWEEPS, dtype=jnp.int32))
    trace_blocks = traces.reshape(SWEEPS, SEG, N_CHAN, block_width).transpose(2, 0, 1, 3)
    shot_of = sweep_table[1]
    member = (shot_of[:, None] == jnp.arange(SHOTS, dtype=jnp.int32)[None, :]).astype(jnp.float32)
    member_half = member.astype(jnp.bfloat16)
    counts = jnp.sum(member, axis=0)

    def first_stack(trace_block):
        summed = jnp.dot(member_half.T, trace_block.reshape(SWEEPS, SEG * block_width), preferred_element_type=jnp.float32)
        return summed.reshape(SHOTS, SEG, block_width) / counts[:, None, None]

    stack_blocks = lax.map(first_stack, trace_blocks)

    def energy_block(pair):
        trace_block, stack_block = pair
        fitted = stack_block[shot_of]
        return jnp.mean(jnp.square(trace_block.astype(jnp.float32) - fitted), axis=1)

    for iteration in range(ITERS):
        energies = lax.map(energy_block, (trace_blocks, stack_blocks))
        spread = jnp.sum(energies) / (SWEEPS * CHANNELS) + EPSILON

        def update_block(pair, spread=spread):
            trace_block, energy = pair
            weight = 1.0 / (1.0 + energy / spread)
            weighted = weight[:, None, :] * trace_block.astype(jnp.float32)
            numerator = jnp.einsum("gk,guc->kuc", member, weighted, precision=lax.Precision.HIGHEST)
            denominator = jnp.dot(member.T, weight, precision=lax.Precision.HIGHEST)
            return numerator / denominator[:, None, :]

        stack_blocks = lax.map(update_block, (trace_blocks, energies))
    stacked = stack_blocks.transpose(1, 2, 0, 3).reshape(SHOTS, SEG, CHANNELS)
    return jnp.zeros_like(stacked).at[owner_map].set(stacked)
```

```python
import functools

import jax
import jax.numpy as jnp
from jax import lax
from jax.experimental import pallas as pl
from jax.experimental.pallas import tpu as pltpu
from jax.sharding import PartitionSpec as P

SEG = 1024
ITERS = 3
EPSILON = 1e-06
MESH = pl.DeviceIdType.MESH
LANES = 128


def passed_along(value, axis, steps):
    count = lax.axis_size(axis)
    first, last = (max(0, -steps), min(count, count - steps))
    return lax.ppermute(value, axis, [(source, source + steps) for source in range(first, last)])


def template_kernel(offset_ref, pilot_ref, out_ref):
    rows, width = out_ref.shape
    offset = offset_ref[0]
    base = jnp.broadcast_to(pilot_ref[...], (8, width))
    base = pltpu.roll(base, 0, 1, stride=1, stride_axis=0)

    @pl.loop(0, rows // 16)
    def _(group):
        shift = offset + group * 16
        first = pltpu.roll(base, shift, 1)
        second = pltpu.roll(base, shift + 8, 1)
        block = jnp.concatenate([first, second], axis=0)
        out_ref[pl.ds(pl.multiple_of(group * 16, 16), 16), :] = block.astype(out_ref.dtype)


def template(pilot_sweep, offset, rows, slack):
    length = pilot_sweep.shape[0]
    width = length + slack + rows
    padded = jnp.pad(pilot_sweep.astype(jnp.float32), (0, width - length))[None, :]
    return pl.pallas_call(
        template_kernel,
        out_shape=jax.ShapeDtypeStruct((rows, width), jnp.bfloat16),
        in_specs=[
            pl.BlockSpec(memory_space=pltpu.SMEM),
            pl.BlockSpec(memory_space=pltpu.VMEM),
        ],
        out_specs=pl.BlockSpec(memory_space=pltpu.VMEM),
        name="template",
    )(offset.reshape(1), padded)


def stack_kernel(
    n_tm, n_chan, total_count,
    traces, same, place, out,
    dpart, rsbuf, dall, coef, tiles,
    rs_send, rs_recv, ag_send, ag_recv, en_send, en_recv,
):
    sweeps, rows, channels = traces.shape
    shots = out.shape[0]
    half_pairs = sweeps // 2
    half = channels // 2
    t = lax.axis_index("tm")
    c = lax.axis_index("chan")

    barrier = pltpu.get_barrier_semaphore()
    for k in range(1, n_tm):
        pl.semaphore_signal(barrier, inc=1, device_id=(lax.rem(t + k, n_tm), c), device_id_type=MESH)
    for k in range(1, n_chan):
        pl.semaphore_signal(barrier, inc=1, device_id=(t, lax.rem(c + k, n_chan)), device_id_type=MESH)

    def sample(g, start, lanes):
        return traces[g, pl.ds(start, 16), lanes].astype(jnp.float32)

    for side in range(2):

        @pl.loop(0, half // LANES)
        def _(chunk):
            lanes = pl.ds(pl.multiple_of(side * half + chunk * LANES, LANES), LANES)
            inner = pl.ds(pl.multiple_of(chunk * LANES, LANES), LANES)

            group = sweeps if sweeps <= 8 else 2
            for g0 in range(0, sweeps, group):
                totals = {}
                for start in range(0, rows, 16):
                    held = {}
                    for g in range(g0, g0 + group):
                        for d in range(1, half_pairs + 1):
                            if d == half_pairs and g >= half_pairs:
                                continue
                            ends = (g, (g + d) % sweeps)
                            for end in ends:
                                if end not in held:
                                    held[end] = sample(end, start, lanes)
                            gap = held[ends[0]] - held[ends[1]]
                            gap = gap * gap
                            gap = gap[:8] + gap[8:]
                            totals[g, d] = totals[g, d] + gap if start else gap
                for (g, d), total in totals.items():
                    row = jnp.sum(total, axis=0, keepdims=True)
                    dpart[2 * d - 2 + side, g:g + 1, inner] = row
                    if d == half_pairs:
                        dpart[2 * d - 2 + side, g + d:g + d + 1, inner] = row

    pl.semaphore_wait(barrier, n_tm - 1 + n_chan - 1)

    def rs_copy(k):
        peer = lax.rem(t + k, n_tm)
        return pltpu.make_async_remote_copy(
            src_ref=dpart.at[peer], dst_ref=rsbuf.at[t],
            send_sem=rs_send.at[peer], recv_sem=rs_recv.at[t],
            device_id=(peer, c), device_id_type=MESH,
        )

    def rs_arrival(k):
        peer = lax.rem(t + k, n_tm)
        return pltpu.make_async_remote_copy(
            src_ref=dpart.at[peer], dst_ref=rsbuf.at[peer],
            send_sem=rs_send.at[peer], recv_sem=rs_recv.at[peer],
            device_id=(peer, c), device_id_type=MESH,
        )

    for k in range(1, n_tm):
        rs_copy(k).start()
    rsbuf[t] = dpart[t]
    for k in range(1, n_tm):
        rs_arrival(k).wait_recv()
    total = rsbuf[0]
    for k in range(1, n_tm):
        total = total + rsbuf[k]
    dall[t] = total

    def ag_copy(k):
        peer = lax.rem(t + k, n_tm)
        return pltpu.make_async_remote_copy(
            src_ref=dall.at[t], dst_ref=dall.at[t],
            send_sem=ag_send.at[peer], recv_sem=ag_recv.at[t],
            device_id=(peer, c), device_id_type=MESH,
        )

    def ag_arrival(k):
        peer = lax.rem(t + k, n_tm)
        return pltpu.make_async_remote_copy(
            src_ref=dall.at[peer], dst_ref=dall.at[peer],
            send_sem=ag_send.at[peer], recv_sem=ag_recv.at[peer],
            device_id=(peer, c), device_id_type=MESH,
        )

    for k in range(1, n_tm):
        ag_copy(k).start()
    for k in range(1, n_tm):
        ag_arrival(k).wait_recv()

    masks = [same[d][:, 0:1] for d in range(half_pairs)]

    def ahead(value, d):
        return pltpu.roll(value, sweeps - d, 0)

    def behind(value, d):
        return pltpu.roll(value, d, 0)

    def over_shot(value):
        result = value
        for d in range(1, half_pairs + 1):
            result = result + masks[d - 1] * ahead(value, d)
            if d < half_pairs:
                result = result + behind(masks[d - 1] * value, d)
        return result

    def pair(d, side):
        return masks[d - 1] * dall[2 * (d - 1) + side]

    def energy_of(weight, side):
        spent = jnp.zeros_like(weight)
        for d in range(1, half_pairs + 1):
            gaps = pair(d, side)
            spent = spent + gaps * ahead(weight, d)
            if d < half_pairs:
                spent = spent + behind(gaps * weight, d)
        scale = 1.0 / over_shot(weight)
        energy = spent * scale - 0.5 * over_shot(weight * spent) * (scale * scale)
        return jnp.maximum(energy, 0.0) / SEG

    weights = [jnp.ones((sweeps, half), jnp.float32) for _ in range(2)]
    for iteration in range(ITERS):
        energies = [energy_of(weights[side], side) for side in range(2)]
        part = jnp.zeros((sweeps, LANES), jnp.float32)
        for side in range(2):
            for chunk in range(half // LANES):
                part = part + energies[side][:, chunk * LANES:(chunk + 1) * LANES]
        tiles[iteration, c] = part

        def en_copy(k, iteration=iteration):
            peer = lax.rem(c + k, n_chan)
            return pltpu.make_async_remote_copy(
                src_ref=tiles.at[iteration, c], dst_ref=tiles.at[iteration, c],
                send_sem=en_send.at[iteration, peer], recv_sem=en_recv.at[iteration, c],
                device_id=(t, peer), device_id_type=MESH,
            )

        def en_arrival(k, iteration=iteration):
            peer = lax.rem(c + k, n_chan)
            return pltpu.make_async_remote_copy(
                src_ref=tiles.at[iteration, peer], dst_ref=tiles.at[iteration, peer],
                send_sem=en_send.at[iteration, peer], recv_sem=en_recv.at[iteration, peer],
                device_id=(t, peer), device_id_type=MESH,
            )

        for k in range(1, n_chan):
            en_copy(k).start()
        for k in range(1, n_chan):
            en_arrival(k).wait_recv()
        everything = tiles[iteration, 0]
        for k in range(1, n_chan):
            everything = everything + tiles[iteration, k]
        everything = jnp.sum(jnp.sum(everything, axis=1, keepdims=True), axis=0, keepdims=True)
        spread = everything / total_count + EPSILON
        weights = [1.0 / (1.0 + energies[side] / spread) for side in range(2)]
        for k in range(1, n_chan):
            en_copy(k).wait_send()

    for side in range(2):
        share = weights[side] / over_shot(weights[side])
        for q in range(shots):
            coef[q, :, side * half:(side + 1) * half] = place[q][:, 0:1] * share

    @pl.loop(0, channels // LANES)
    def _(chunk):
        lanes = pl.ds(pl.multiple_of(chunk * LANES, LANES), LANES)
        for q0 in range(0, shots, 2):
            rates = [[coef[q, g:g + 1, lanes] for g in range(sweeps)] for q in range(q0, min(q0 + 2, shots))]

            @pl.loop(0, rows // 16)
            def _(group):
                start = pl.multiple_of(group * 16, 16)
                sums = [jnp.zeros((16, LANES), jnp.float32) for _ in rates]
                for g in range(sweeps):
                    value = sample(g, start, lanes)
                    for q, rate in enumerate(rates):
                        sums[q] = sums[q] + rate[g] * value
                for q in range(len(rates)):
                    out[q0 + q, pl.ds(start, 16), lanes] = sums[q]

    for k in range(1, n_tm):
        rs_copy(k).wait_send()
        ag_copy(k).wait_send()


def robust_stack(traces, sweep_table, owner_map):
    sweeps, rows, channels = traces.shape
    shots = owner_map.shape[0]
    n_tm, n_chan = lax.axis_size("tm"), lax.axis_size("chan")
    half_pairs = sweeps // 2
    shot = sweep_table[1]
    same = jnp.stack([shot == jnp.roll(shot, -d) for d in range(1, half_pairs + 1)])
    same = jnp.broadcast_to(same.astype(jnp.float32)[:, :, None], (half_pairs, sweeps, LANES))
    place = owner_map[shot][None, :] == jnp.arange(shots, dtype=jnp.int32)[:, None]
    place = jnp.broadcast_to(place.astype(jnp.float32)[:, :, None], (shots, sweeps, LANES))
    total_count = sweeps * channels * n_chan
    return pl.pallas_call(
        functools.partial(stack_kernel, n_tm, n_chan, total_count),
        out_shape=jax.ShapeDtypeStruct((shots, rows, channels), jnp.float32),
        in_specs=[pl.BlockSpec(memory_space=pltpu.VMEM)] * 3,
        out_specs=pl.BlockSpec(memory_space=pltpu.VMEM),
        scratch_shapes=[
            pltpu.VMEM((sweeps, sweeps, channels // 2), jnp.float32),
            pltpu.VMEM((sweeps, sweeps, channels // 2), jnp.float32),
            pltpu.VMEM((sweeps, sweeps, channels // 2), jnp.float32),
            pltpu.VMEM((shots, sweeps, channels), jnp.float32),
            pltpu.VMEM((ITERS, n_chan, sweeps, LANES), jnp.float32),
            pltpu.SemaphoreType.DMA((n_tm,)),
            pltpu.SemaphoreType.DMA((n_tm,)),
            pltpu.SemaphoreType.DMA((n_tm,)),
            pltpu.SemaphoreType.DMA((n_tm,)),
            pltpu.SemaphoreType.DMA((ITERS, n_chan)),
            pltpu.SemaphoreType.DMA((ITERS, n_chan)),
        ],
        compiler_params=pltpu.CompilerParams(
            collective_id=0, has_side_effects=True, vmem_limit_bytes=40 * 2**20
        ),
        name="robust_stack",
    )(traces, same, place)


def shards(record, pilot_sweep, sweep_table, owner_map):
    block_rows, channels = record.shape
    n_tm = lax.axis_size("tm")
    length = pilot_sweep.shape[0]
    slack = block_rows - length
    step = 256
    following = passed_along(record[:SEG], "tm", -1)
    joined = jnp.concatenate([record, following], axis=0)
    here = lax.axis_index("tm")
    column = lax.dynamic_slice_in_dim(sweep_table, here, 1, 1)[:, 0]
    offset = column[0] - here * block_rows
    polarity = 1.0 - 2.0 * (column[2] % 2).astype(jnp.float32)
    taps = template(pilot_sweep * polarity.astype(jnp.bfloat16), offset, step, slack)
    pieces = [
        jnp.dot(taps, joined[s:s + taps.shape[1]], preferred_element_type=jnp.float32).astype(jnp.bfloat16)
        for s in range(0, SEG, step)
    ]
    traces = jnp.concatenate(pieces, axis=0).reshape(n_tm, SEG // n_tm, channels)
    arrived = lax.all_to_all(traces, "tm", split_axis=0, concat_axis=0, tiled=True)
    return robust_stack(arrived, sweep_table, owner_map)


def solution(mesh):
    placed = (P("tm", "chan"), P(), P(), P())
    return jax.shard_map(
        shards, mesh=mesh, in_specs=placed, out_specs=P(None, "tm", "chan"), check_vma=False
    )
```
